32 devices in a mesh: dyn: 4 (over x, core), col: 8 (over z, y).
Axes of the slice: x: 2, y: 2, z: 4, core: 2. Of those that a mesh axis runs over, the one named last changes fastest.
Arguments:
- planck_source: float32 [32, 32768], P(None, ('dyn', 'col')), may hold values from 0.5 to 1.5
- absorber_path: float32 [32, 32768], P(None, ('dyn', 'col')), may hold values from 0.2 to 3
- cloud_depth: float32 [32, 32768], P(None, ('dyn', 'col')), may hold values from 0 to 0.6
- span_map: int32 [32768], P(('dyn', 'col')), may hold values from 0 to 32767, as said below
- surface_source: float32 [32768], P(('dyn', 'col')), may hold values from 0.8 to 1.6
- interp_index: int32 [32, 32768], P(None, ('dyn', 'col')), may hold values from 0 to 830
- interp_weight: bfloat16 [4, 32, 32768], P(None, None, ('dyn', 'col')), may hold values from 0 to 0.5
- sunlit: int32 [32768], P(('dyn', 'col')), may hold values from 0 to 1, as said below
- sw_slot: int32 [32768], P(('dyn', 'col')), may hold values from 0 to 4095, as said below
- cos_zenith: float32 [32768], P(('dyn', 'col')), may hold values from 0.05 to 1
- albedo: float32 [32768], P(('dyn', 'col')), may hold values from 0.05 to 0.8
- table_lw: bfloat16 [256, 896], replicated, may hold values from 0.0029907227 to 3
- table_sw: bfloat16 [224, 896], replicated, may hold values from 0.0029 to 3
- planck_frac: float32 [256], replicated, may hold values from 0.0001 to 0.02
- solar_weight: float32 [224], replicated, may hold values from 0.0001 to 0.02
Outputs:
- heating_lw: float32 [32, 32768], P(None, ('dyn', 'col'))
- heating_sw: float32 [32, 32768], P(None, ('dyn', 'col'))
- sw_surface: float32 [16384], P(('dyn', 'col'))
The draws below stay inside these ranges and needn't reach their ends.
Inputs may be any that keep to these rules, and one draw needn't show every extreme that they name: A permutation of the 32768 physics columns: column i goes to device span_map[i] // 1024 (flat index dyn * 8 + col), position span_map[i] % 1024. The number of columns that device s sends to device t depends only on (t - s) modulo the number of devices, is at most 64, and equals 64 for some pairs. In each dyn row the devices fall into pairs whose sunlit counts add up to 1024, so a dyn row holds 4096 sunlit columns; in every dyn row some device is sunlit in all its columns. For a sunlit column, sw_slot // 512 is the col index of the device of its dyn row that computes its shortwave and sw_slot % 512 its slot there. The sunlit columns of a dyn row, in order of device and column, are dealt to owners in turn from a drawn start; the values are distinct, every owner gets exactly 512, at most 128 from any one device and exactly that many from a fully sunlit one. For dark columns the value is arbitrary.
All inputs are finite; a program needn't handle non-finite values.
Results may differ from the reference program's by a relative error of at most 0.0003.
Values may be sent and summed in bfloat16 or wider, within the bound.
A program may use at most 128 MiB of HBM per device.

```python
import math
from functools import partial
import jax
import jax.numpy as jnp
from jax import lax

G_LW = 256
G_SW = 224
TEMPS = 14
PRESS = 64
LEV = 32
COL_DEV = 1024
NTAB = 896
COLS = 32768
CAP = 64
SW_DEV = 512
SW_ALL = 16384
N_DYN = 4
N_COL = 8


def shuffled(key, groups, length):
    return jax.vmap(lambda group_key: jax.random.permutation(group_key, length))(jax.random.split(key, groups)).astype(jnp.int32)


def daylight(key):
    subkeys = jax.random.split(key, 6)
    stripes = N_COL
    half_cols = COL_DEV // 2
    shuffle = shuffled(subkeys[0], N_DYN, stripes)
    excess = jax.random.randint(subkeys[1], (N_DYN, stripes // 2), 0, half_cols + 1).astype(jnp.int32)
    excess = excess.at[:, 0].set(half_cols)
    row_ids = jnp.arange(N_DYN, dtype=jnp.int32)[:, None]
    counts = jnp.zeros((N_DYN, stripes), jnp.int32)
    counts = counts.at[row_ids, shuffle[:, :stripes // 2]].set(half_cols + excess)
    counts = counts.at[row_ids, shuffle[:, stripes // 2:]].set(half_cols - excess)
    rank_of = shuffled(subkeys[2], N_DYN * stripes, COL_DEV).reshape(N_DYN, stripes, COL_DEV)
    lighted = (rank_of < counts[:, :, None]).astype(jnp.int32)
    flattened = lighted.reshape(N_DYN, stripes * COL_DEV)
    dealt_rank = jnp.clip(jnp.cumsum(flattened, axis=1) - 1, 0, None)
    offset = jax.random.randint(subkeys[3], (N_DYN, 1), 0, stripes).astype(jnp.int32)
    holder = (dealt_rank + offset) % stripes
    turn_of = jnp.minimum(dealt_rank // stripes, SW_DEV - 1)
    slot_perm = shuffled(subkeys[4], N_DYN * stripes, SW_DEV).reshape(N_DYN, stripes, SW_DEV)
    chosen = slot_perm[row_ids, holder, turn_of]
    filler_slots = jax.random.randint(subkeys[5], (N_DYN, stripes * COL_DEV), 0, stripes * SW_DEV).astype(jnp.int32)
    pairing = jnp.where(flattened == 1, holder * SW_DEV + chosen, filler_slots)
    return (flattened.reshape(-1).astype(jnp.int32), pairing.reshape(-1).astype(jnp.int32))


def draw_sunlit(key, part):
    lighted, pairing = daylight(key)
    return lighted


def draw_sw_slot(key, part):
    lighted, pairing = daylight(key)
    return pairing


def draw_span_map(key, part):
    key = jax.random.fold_in(key, 7)
    subkeys = jax.random.split(key, 4)
    devices = N_DYN * N_COL
    shares = jax.random.randint(subkeys[0], (devices // 2,), 0, CAP + 1).astype(jnp.int32)
    shares = shares.at[0].set(CAP)
    pattern = jnp.stack([shares, CAP - shares], axis=1).reshape(devices)
    pattern = pattern[jax.random.permutation(subkeys[1], devices)]
    senders = jnp.arange(devices, dtype=jnp.int32)
    counts = pattern[(senders[None, :] - senders[:, None]) % devices]
    upper_edge = jnp.cumsum(counts, axis=1)
    column = jnp.arange(COL_DEV, dtype=jnp.int32)
    target = jnp.sum((upper_edge[:, None, :] <= column[None, :, None]).astype(jnp.int32), axis=2)
    within = column[None, :] - jnp.take_along_axis(upper_edge - counts, target, axis=1)
    before = jnp.cumsum(counts, axis=0) - counts
    arrival = jnp.take_along_axis(before, target, axis=1) + within
    landing = shuffled(subkeys[2], devices, COL_DEV)
    placed_at = landing[target, arrival]
    global_slot = target * COL_DEV + placed_at
    mixing = shuffled(subkeys[3], devices, COL_DEV)
    mapped = jnp.take_along_axis(global_slot, mixing, axis=1)
    return mapped.reshape(-1).astype(jnp.int32)


def draw_cloud_depth(key, part):
    key = jax.random.fold_in(key, 11)
    level_key, column_key = jax.random.split(key, 2)
    layer = jax.random.uniform(level_key, (LEV, COLS), jnp.float32, 0.0, 0.6)
    factor = jnp.exp(jax.random.uniform(column_key, (COLS,), jnp.float32, jnp.log(0.01), 0.0))
    return (layer * factor[None, :]).astype(jnp.float32)


def draw_table_sw(key, part):
    key = jax.random.fold_in(key, 13)
    row_key, entry_key = jax.random.split(key, 2)
    floor_value = 0.003
    top = jnp.exp(jax.random.uniform(row_key, (G_SW, 1), jnp.float32, jnp.log(0.005), jnp.log(3.0)))
    spread = jax.random.uniform(entry_key, (G_SW, TEMPS * PRESS), jnp.float32, 0.0, 1.0)
    table = jnp.exp(jnp.log(floor_value) + (jnp.log(top) - jnp.log(floor_value)) * spread)
    return jnp.clip(table, floor_value, 3.0).astype(jnp.bfloat16)


def touch_ends(array, rng, smallest, top_value):
    index_at = [jax.random.randint(jax.random.fold_in(rng, axis), (), 0, length) for axis, length in enumerate(array.shape)]
    longest = array.shape.index(max(array.shape))
    beside = index_at[:longest] + [(index_at[longest] + 1) % array.shape[longest]] + index_at[longest + 1:]
    return array.at[tuple(index_at)].set(smallest).at[tuple(beside)].set(top_value)


def steps_of(own_key, shape, cuts, low, largest):
    gain = 1.0
    for position, shards_of in cuts:
        steps = jax.random.uniform(jax.random.fold_in(jax.random.fold_in(own_key, 6), position), (shards_of,), jnp.float32, low / len(cuts), largest / len(cuts))
        gain = gain * jnp.repeat(jnp.exp(steps), shape[position] // shards_of).reshape((-1,) + (1,) * (len(shape) - 1 - position))
    return gain


def setup_inputs(seed: int = 0) -> dict:
    streams_of = jax.random.split(jax.random.key(seed), 16)
    return {
        "planck_source": jnp.clip(0.5 + 1.0 * jax.random.uniform(streams_of[0], (LEV, COLS), jnp.float32) ** steps_of(streams_of[0], (LEV, COLS), ((1, 32),), -0.2, 0.2), 0.5, 1.5),
        "absorber_path": jnp.clip(jnp.exp(math.log(3.0) - 2.7080502 * jax.random.uniform(streams_of[1], (LEV, COLS), jnp.float32) ** steps_of(streams_of[1], (LEV, COLS), ((1, 32),), -0.2, 0.2)), 0.2, 3.0),
        "cloud_depth": draw_cloud_depth(jax.random.fold_in(streams_of[15], 71), 0),
        "span_map": draw_span_map(jax.random.fold_in(streams_of[15], 71), 0),
        "surface_source": jnp.clip(0.8 + 0.8 * jax.random.uniform(streams_of[4], (COLS,), jnp.float32) ** steps_of(streams_of[4], (COLS,), ((0, 32),), -0.2, 0.2), 0.8, 1.6),
        "interp_index": touch_ends(jax.random.randint(streams_of[5], (LEV, COLS), 0, (TEMPS - 1) * PRESS - 1), jax.random.fold_in(streams_of[5], 1), 0, ((TEMPS - 1) * PRESS - 1) - 1).astype(jnp.int32),
        "interp_weight": jnp.clip(0.5 * jax.random.uniform(streams_of[6], (4, LEV, COLS), jnp.float32) ** steps_of(streams_of[6], (4, LEV, COLS), ((2, 32),), -0.2, 0.2), 0.0, 0.5).astype(jnp.bfloat16),
        "sunlit": draw_sunlit(jax.random.fold_in(streams_of[15], 71), 0),
        "sw_slot": draw_sw_slot(jax.random.fold_in(streams_of[15], 71), 0),
        "cos_zenith": jnp.clip(0.05 + 0.95 * jax.random.uniform(streams_of[9], (COLS,), jnp.float32) ** steps_of(streams_of[9], (COLS,), ((0, 32),), -0.2, 0.2), 0.05, 1.0),
        "albedo": jnp.clip(0.05 + 0.75 * jax.random.uniform(streams_of[10], (COLS,), jnp.float32) ** steps_of(streams_of[10], (COLS,), ((0, 32),), -0.2, 0.2), 0.05, 0.8),
        "table_lw": jnp.clip(jnp.exp(jax.random.uniform(streams_of[11], (G_LW, NTAB), jnp.float32, math.log(0.0029907227), math.log(3.0))), 0.0029907227, 3.0).astype(jnp.bfloat16),
        "table_sw": draw_table_sw(jax.random.fold_in(streams_of[15], 71), 0),
        "planck_frac": jnp.clip(jnp.exp(jax.random.uniform(streams_of[13], (G_LW,), jnp.float32, math.log(0.0001), math.log(0.02))), 0.0001, 0.02),
        "solar_weight": jnp.clip(jnp.exp(jax.random.uniform(streams_of[14], (G_SW,), jnp.float32, math.log(0.0001), math.log(0.02))), 0.0001, 0.02),
    }


def corner_weights(index_row, weight_rows):
    entries = jnp.arange(TEMPS * PRESS, dtype=jnp.int32)[:, None]
    offsets = (0, 1, PRESS, PRESS + 1)
    mixing = jnp.zeros((TEMPS * PRESS, index_row.shape[0]), jnp.bfloat16)
    for corner in range(4):
        matches = entries == (index_row[None, :] + offsets[corner])
        mixing = mixing + jnp.where(matches, weight_rows[corner][None, :], jnp.zeros((), jnp.bfloat16))
    return mixing


def optical_depth(table, index_row, weight_rows, path_row, cloud_row):
    absorb = jnp.dot(table, corner_weights(index_row, weight_rows), preferred_element_type=jnp.float32)
    return path_row[None, :] * absorb + cloud_row[None, :]


def longwave(table, planck_frac, index_cols, weight_cols, path_cols, cloud_cols, planck_cols, surface_cols):
    fraction = planck_frac[:, None]
    weight_levels = jnp.moveaxis(weight_cols, 0, 1)

    def downward(flux_in, inputs):
        index_row, weight_rows, path_row, cloud_row, planck_row = inputs
        optical = optical_depth(table, index_row, weight_rows, path_row, cloud_row)
        transmit = jnp.exp(-1.66 * optical)
        flux_out = flux_in * transmit + fraction * planck_row[None, :] * (1.0 - transmit)
        return flux_out, (transmit, jnp.sum(flux_in - flux_out, axis=0))

    initial = jnp.zeros((table.shape[0], index_cols.shape[1]), jnp.float32)
    bottom_down, (transmits, gained_down) = lax.scan(downward, initial, (index_cols, weight_levels, path_cols, cloud_cols, planck_cols))

    def upward(flux_in, inputs):
        transmit, planck_row = inputs
        flux_out = flux_in * transmit + fraction * planck_row[None, :] * (1.0 - transmit)
        return flux_out, jnp.sum(flux_in - flux_out, axis=0)

    ground = fraction * surface_cols[None, :]
    top_up, gained_up = lax.scan(upward, ground, (transmits, planck_cols), reverse=True)
    return gained_down + gained_up


def shortwave(table, solar_weight, index_cols, weight_cols, path_cols, cloud_cols, cosine_cols, albedo_cols):
    weight_levels = jnp.moveaxis(weight_cols, 0, 1)

    def downward(beam_in, inputs):
        index_row, weight_rows, path_row, cloud_row = inputs
        optical = optical_depth(table, index_row, weight_rows, path_row, cloud_row)
        beam_out = beam_in * jnp.exp(-optical / cosine_cols[None, :])
        return beam_out, (jnp.exp(-1.66 * optical), jnp.sum(beam_in - beam_out, axis=0))

    initial = solar_weight[:, None] * cosine_cols[None, :]
    ground_beam, (diffuse, gained_down) = lax.scan(downward, initial, (index_cols, weight_levels, path_cols, cloud_cols))

    def upward(flux_in, transmit):
        flux_out = flux_in * transmit
        return flux_out, jnp.sum(flux_in - flux_out, axis=0)

    top_up, gained_up = lax.scan(upward, albedo_cols[None, :] * ground_beam, diffuse, reverse=True)
    ground_gain = jnp.sum(ground_beam, axis=0) * (1.0 - albedo_cols)
    return gained_down + gained_up, ground_gain


def by_blocks(function, arrays, block_cols):
    block_count = arrays[0].shape[-1] // block_cols

    def to_blocks(values):
        shaped = values.reshape(values.shape[:-1] + (block_count, block_cols))
        return jnp.moveaxis(shaped, -2, 0)

    def from_blocks(values):
        joined = jnp.moveaxis(values, 0, -2)
        return joined.reshape(joined.shape[:-2] + (block_count * block_cols,))

    results = lax.map(lambda block_args: function(*block_args), tuple(to_blocks(values) for values in arrays))
    return jax.tree.map(from_blocks, results)


def reference(planck_source, absorber_path, cloud_depth, span_map, surface_source, interp_index, interp_weight, sunlit, sw_slot, cos_zenith, albedo, table_lw, table_sw, planck_frac, solar_weight):
    total_cols = span_map.shape[0]
    anchor = jnp.zeros((total_cols,), jnp.int32).at[span_map].set(jnp.arange(total_cols, dtype=jnp.int32))
    planck_phys = jnp.take(planck_source, anchor, axis=1)
    path_phys = jnp.take(absorber_path, anchor, axis=1)
    cloud_phys = jnp.take(cloud_depth, anchor, axis=1)
    lw_heat = by_blocks(partial(longwave, table_lw, planck_frac), (interp_index, interp_weight, path_phys, cloud_phys, planck_phys, surface_source), min(512, COL_DEV))
    row_of = jnp.arange(total_cols, dtype=jnp.int32) // (N_COL * COL_DEV)
    target = jnp.where(sunlit == 1, row_of * (N_COL * SW_DEV) + sw_slot, SW_ALL).astype(jnp.int32)
    chosen = jnp.full((SW_ALL,), total_cols, jnp.int32).at[target].set(jnp.arange(total_cols, dtype=jnp.int32), mode="drop")
    sw_inputs = tuple(jnp.take(values, chosen, axis=-1) for values in (interp_index, interp_weight, path_phys, cloud_phys, cos_zenith, albedo))
    sw_heat, sw_surface = by_blocks(partial(shortwave, table_sw, solar_weight), sw_inputs, min(512, SW_DEV))
    sw_phys = jnp.take(sw_heat, target, axis=1, mode="fill", fill_value=0.0)
    heating_lw = jnp.take(lw_heat, span_map, axis=1)
    heating_sw = jnp.take(sw_phys, span_map, axis=1)
    return heating_lw, heating_sw, sw_surface
```

```python
import functools
import math

import jax
import jax.numpy as jnp
from jax import lax
from jax.experimental import pallas as pl
from jax.experimental.pallas import tpu as pltpu
from jax.sharding import PartitionSpec as P

TEMPS = 14
PRESS = 64
LANES = 128
WIDE = 256
AXES = ("dyn", "col")
LOG2E = math.log2(math.e)
DIFFUSE = -1.66 * LOG2E
VMEM = pl.BlockSpec(memory_space=pltpu.VMEM)


def iota(shape, dim):
    return lax.broadcasted_iota(jnp.int32, shape, dim)


def hot(mask):
    return jnp.where(mask, 1.0, 0.0).astype(jnp.bfloat16)


def contract(a, b, dims):
    return lax.dot_general(a, b, (dims, ((), ())), preferred_element_type=jnp.float32)


def pieces(values):
    high = values.astype(jnp.bfloat16)
    rest = values - high.astype(jnp.float32)
    middle = rest.astype(jnp.bfloat16)
    low = (rest - middle.astype(jnp.float32)).astype(jnp.bfloat16)
    return high, middle, low


def plan_kernel(devices, capacity, span_ref, label_ref, place_ref):
    columns = span_ref.shape[1]
    span = span_ref[...]
    target = span >> (columns.bit_length() - 1)
    where = span & (columns - 1)
    marked = target == iota((devices, columns), 0)
    before = hot(iota((columns, columns), 0) < iota((columns, columns), 1))
    counts = contract(hot(marked), before, ((1,), (0,)))
    rank = jnp.sum(jnp.where(marked, counts, 0.0), axis=0, keepdims=True).astype(jnp.int32)
    place_ref[...] = target * capacity + rank
    ranked = hot(rank == iota((LANES, columns), 0))
    high = jnp.where(marked, ((where >> 5) + 1).astype(jnp.float32), 0.0).astype(jnp.bfloat16)
    low = jnp.where(marked, (where & 31).astype(jnp.float32), 0.0).astype(jnp.bfloat16)
    dims = ((1,), (1,))
    label_ref[...] = contract(high, ranked, dims) * 32.0 + contract(low, ranked, dims) - 32.0


def pack_kernel(
    devices, capacity, label_ref, index_ref, weight_ref, surface_ref, cosine_ref, albedo_ref,
    sunlit_ref, slot_ref, out_ref, rows, chosen,
):
    columns = index_ref.shape[1]
    levels = index_ref.shape[0]
    base = 6 * levels
    index = index_ref[...]
    rows[0 : 4 * levels, :] = weight_ref[...]
    rows[4 * levels : 5 * levels, :] = (index >> 6).astype(jnp.float32).astype(jnp.bfloat16)
    rows[5 * levels : 6 * levels, :] = (index & (PRESS - 1)).astype(jnp.float32).astype(jnp.bfloat16)
    slot = slot_ref[...]
    scalars = [
        *pieces(surface_ref[...]),
        *pieces(cosine_ref[...]),
        *pieces(albedo_ref[...]),
        sunlit_ref[...].astype(jnp.float32).astype(jnp.bfloat16),
        (slot >> 7).astype(jnp.float32).astype(jnp.bfloat16),
        (slot & (LANES - 1)).astype(jnp.float32).astype(jnp.bfloat16),
    ]
    scalars = [values.astype(jnp.float32) for values in scalars]
    blank = jnp.zeros((16 - len(scalars), columns), jnp.float32)
    rows[base : base + 16, :] = jnp.concatenate(scalars + [blank], axis=0).astype(jnp.bfloat16)
    rows[base + 16 :, :] = jnp.zeros((WIDE - base - 16, columns), jnp.bfloat16)
    labels = label_ref[...]
    if devices < LANES:
        labels = jnp.concatenate(
            [labels, jnp.zeros((LANES - devices, LANES), jnp.float32)], axis=0
        )
    asked = jnp.transpose(labels).astype(jnp.int32)
    position = iota((capacity, columns), 1)
    for sender in range(devices):
        match = asked[0:capacity, sender : sender + 1] == position
        chosen[sender * capacity : (sender + 1) * capacity, :] = hot(match)
    out_ref[...] = contract(chosen[...], rows[...], ((1,), (1,))).astype(jnp.bfloat16)


def radiation_kernel(
    row_slots, arrived_ref, place_ref, span_ref, path_ref, cloud_ref, planck_ref,
    table_lw_ref, table_sw_ref, frac_ref, solar_ref, lw_ref, sw_ref, surface_ref,
    column_ref, beam_t, diffuse_t, long_t, sum_a, sum_b, ground_ref,
):
    levels, columns = path_ref.shape
    g_lw, g_sw = table_lw_ref.shape[0], table_sw_ref.shape[0]
    slots = arrived_ref.shape[0]
    part = 512
    place = place_ref[...]
    total = None
    for start in range(0, slots, part):
        here = hot(place == iota((part, columns), 0) + start)
        term = contract(arrived_ref[start : start + part, :], here, ((0,), (0,)))
        total = term if total is None else total + term
    column_ref[...] = total
    base = 6 * levels
    tile = WIDE
    table = jnp.concatenate([table_lw_ref[...], table_sw_ref[...]], axis=0)

    def scalar(offset, count, cols):
        values = column_ref[base + offset : base + offset + 1, cols]
        for piece in range(1, count):
            values = values + column_ref[base + offset + piece : base + offset + piece + 1, cols]
        return values

    def column_tile(step, carry):
        cols = pl.ds(pl.multiple_of(step * tile, tile), tile)
        surface = scalar(0, 3, cols)
        cosine = scalar(3, 3, cols)
        albedo = scalar(6, 3, cols)
        sunlit = scalar(9, 1, cols)
        slant = -LOG2E / cosine
        entry = iota((PRESS, tile), 0)

        def absorb_level(level, carry):
            def row(first):
                return column_ref[pl.ds(first + level, 1), cols]

            w0, w1, w2, w3 = (row(k * levels) for k in range(4))
            press = row(5 * levels).astype(jnp.int32)
            temp = row(4 * levels)
            offset = entry - press
            zero = jnp.zeros((), jnp.float32)
            near = jnp.where(offset == 0, w0, jnp.where(offset == 1, w1, zero))
            wrap = offset == 1 - PRESS
            far = jnp.where(
                offset == 0, w2, jnp.where(offset == 1, w3, jnp.where(wrap, w1, zero))
            )
            last = jnp.where(wrap[0:16], w3, zero).astype(jnp.bfloat16)
            near = near.astype(jnp.bfloat16)
            far = far.astype(jnp.bfloat16)
            temp = jnp.broadcast_to(temp.astype(jnp.bfloat16), (16, tile))
            hits = [temp == jnp.full((), k, jnp.bfloat16) for k in range(TEMPS)]
            blank = jnp.zeros((16, tile), jnp.bfloat16)
            blocks = []
            for k in range(TEMPS):
                for sub in range(0, PRESS, 16):
                    rest = blank
                    if k >= 2 and sub == 0:
                        rest = jnp.where(hits[k - 2], last, rest)
                    if k >= 1:
                        rest = jnp.where(hits[k - 1], far[sub : sub + 16], rest)
                    blocks.append(jnp.where(hits[k], near[sub : sub + 16], rest))
            mixing = jnp.concatenate(blocks, axis=0)
            absorb = jnp.dot(table, mixing, preferred_element_type=jnp.float32)
            path = path_ref[pl.ds(level, 1), cols]
            cloud = cloud_ref[pl.ds(level, 1), cols]
            long_t[level] = jnp.exp2(
                absorb[:g_lw] * (path * DIFFUSE) + cloud * DIFFUSE
            )
            beam_t[level] = jnp.exp2(absorb[g_lw:] * (path * slant) + cloud * slant)
            diffuse_t[level] = jnp.exp2(
                absorb[g_lw:] * (path * DIFFUSE) + cloud * DIFFUSE
            )
            return carry

        lax.fori_loop(0, levels, absorb_level, 0)

        sum_a[...] = jnp.zeros_like(sum_a)
        sum_b[...] = jnp.zeros_like(sum_b)

        def fold(values):
            return jnp.sum(values.reshape(-1, 8, values.shape[-1]), axis=0)

        chunk = 32
        weight_sum = jnp.sum(frac_ref[...])
        planck = planck_ref[:, cols]

        for start in range(0, g_lw, chunk):
            g = slice(start, start + chunk)
            frac = jnp.broadcast_to(frac_ref[g, :], (chunk, tile))

            def planck_row(level):
                return planck_ref[pl.ds(level, 1), cols]

            def down(level, state):
                passed = state * long_t[level, g, :]
                sum_a[level] += fold(passed * frac)
                following = jnp.minimum(level + 1, levels - 1)
                return passed + (planck_row(level) - planck_row(following))

            state = jnp.broadcast_to(-planck_row(0), (chunk, tile))
            lax.fori_loop(0, levels, down, state, unroll=4)

            def up(back, state):
                level = levels - 1 - back
                passed = state * long_t[level, g, :]
                sum_b[level] += fold(passed * frac)
                following = jnp.maximum(level - 1, 0)
                return passed + (planck_row(level) - planck_row(following))

            state = jnp.broadcast_to(surface - planck_row(levels - 1), (chunk, tile))
            lax.fori_loop(0, levels, up, state, unroll=4)

        own = planck * weight_sum
        below = jnp.sum(sum_a[...], axis=1) + own
        above = jnp.sum(sum_b[...], axis=1) + own
        ground = surface * weight_sum
        entering_down = jnp.concatenate([jnp.zeros((1, tile), jnp.float32), below[:-1]], axis=0)
        entering_up = jnp.concatenate([above[1:], ground], axis=0)
        lw_ref[:, cols] = (entering_down - below) + (entering_up - above)

        sum_a[...] = jnp.zeros_like(sum_a)
        sum_b[...] = jnp.zeros_like(sum_b)
        for start in range(0, g_sw, chunk):
            g = slice(start, start + chunk)

            def sun_down(level, state):
                state = state * beam_t[level, g, :]
                sum_a[level] += fold(state)
                return state

            state = jnp.broadcast_to(solar_ref[g, :], (chunk, tile))
            state = lax.fori_loop(0, levels, sun_down, state, unroll=4)

            def sun_up(back, state):
                level = levels - 1 - back
                state = state * diffuse_t[level, g, :]
                sum_b[level] += fold(state)
                return state

            lax.fori_loop(0, levels, sun_up, state, unroll=4)

        beam = jnp.sum(sum_a[...], axis=1) * cosine
        reflect = albedo * cosine
        diffuse = jnp.sum(sum_b[...], axis=1) * reflect
        top = jnp.sum(solar_ref[...]) * cosine
        arriving = jnp.concatenate([top, beam[:-1]], axis=0)
        rising = jnp.concatenate([diffuse[1:], albedo * beam[-1:]], axis=0)
        heat = (arriving - beam) + (rising - diffuse)
        sw_ref[:, cols] = jnp.where(sunlit > 0.5, heat, 0.0)
        ground_ref[:, cols] = jnp.where(sunlit > 0.5, (1.0 - albedo) * beam[-1:], 0.0)
        return carry

    lax.fori_loop(0, columns // tile, column_tile, 0)

    groups = surface_ref.shape[0]
    every = pl.ds(0, columns)
    slot_high = scalar(10, 1, every).astype(jnp.int32)
    slot_low = scalar(11, 1, every).astype(jnp.int32)
    dyn_row = span_ref[...] // row_slots[0]
    home = dyn_row * (row_slots[1] // LANES) + slot_high
    at_home = home == iota((groups, columns), 0)
    at_lane = hot(slot_low == iota((LANES, columns), 0))
    total = None
    for piece in pieces(ground_ref[...]):
        spread = jnp.where(at_home, piece.astype(jnp.float32), 0.0).astype(jnp.bfloat16)
        term = contract(spread, at_lane, ((1,), (1,)))
        total = term if total is None else total + term
    surface_ref[...] = total


def params():
    return pltpu.CompilerParams(vmem_limit_bytes=56 * 1024 * 1024)


def shape_of(shape, dtype):
    return jax.ShapeDtypeStruct(shape, dtype)


def whereabouts():
    stripes = lax.axis_size("col")
    devices = lax.axis_size("dyn") * stripes
    return lax.axis_index("dyn") * stripes + lax.axis_index("col"), stripes, devices


def peer(flat, stripes):
    return (flat // stripes, flat % stripes)


def greet():
    me, stripes, devices = whereabouts()
    barrier = pltpu.get_barrier_semaphore()

    def signal(step, carry):
        pl.semaphore_signal(
            barrier, inc=1, device_id=peer((me + step) % devices, stripes),
            device_id_type=pl.DeviceIdType.MESH,
        )
        return carry

    lax.fori_loop(1, devices, signal, 0)
    pl.semaphore_wait(barrier, devices - 1)


def swap_blocks(source, landing, send, receive, own):
    me, stripes, devices = whereabouts()

    def copy_of(step):
        target = (me + step) % devices
        return pltpu.make_async_remote_copy(
            src_ref=source.at[target], dst_ref=landing.at[me],
            send_sem=send.at[step], recv_sem=receive.at[step],
            device_id=peer(target, stripes), device_id_type=pl.DeviceIdType.MESH,
        )

    def start(step, carry):
        copy_of(step).start()
        return carry

    def finish(step, carry):
        copy_of(step).wait()
        return carry

    kept = pltpu.make_async_copy(source.at[me], landing.at[me], own)
    kept.start()
    lax.fori_loop(1, devices, start, 0)
    lax.fori_loop(1, devices, finish, 0)
    kept.wait()


def swap_kernel(source, landing, send, receive, own):
    greet()
    swap_blocks(source, landing, send, receive, own)


def swap(values, ident):
    devices = values.shape[0]
    return pl.pallas_call(
        swap_kernel,
        out_shape=shape_of(values.shape, values.dtype),
        in_specs=[VMEM],
        out_specs=VMEM,
        scratch_shapes=[
            pltpu.SemaphoreType.DMA((devices,)),
            pltpu.SemaphoreType.DMA((devices,)),
            pltpu.SemaphoreType.DMA,
        ],
        compiler_params=pltpu.CompilerParams(collective_id=ident, has_side_effects=True),
    )(values)


def collect_kernel(source, total, landing, send, receive, own):
    greet()
    swap_blocks(source, landing, send, receive, own)
    total[...] = jnp.sum(landing[...], axis=0)


def collect(values, ident):
    devices = values.shape[0]
    return pl.pallas_call(
        collect_kernel,
        out_shape=shape_of(values.shape[1:], values.dtype),
        in_specs=[VMEM],
        out_specs=VMEM,
        scratch_shapes=[
            pltpu.VMEM(values.shape, values.dtype),
            pltpu.SemaphoreType.DMA((devices,)),
            pltpu.SemaphoreType.DMA((devices,)),
            pltpu.SemaphoreType.DMA,
        ],
        compiler_params=pltpu.CompilerParams(collective_id=ident, has_side_effects=True),
    )(values)


def body(
    planck_source, absorber_path, cloud_depth, span_map, surface_source, interp_index,
    interp_weight, sunlit, sw_slot, cos_zenith, albedo, table_lw, table_sw, planck_frac,
    solar_weight,
):
    levels, columns = planck_source.shape
    stripes = lax.axis_size("col")
    devices = lax.axis_size("dyn") * stripes
    capacity = 2 * columns // devices
    slots = devices * capacity
    span = span_map[None, :]
    labels, place = pl.pallas_call(
        functools.partial(plan_kernel, devices, capacity),
        out_shape=(
            shape_of((devices, LANES), jnp.float32),
            shape_of((1, columns), jnp.int32),
        ),
        in_specs=[VMEM],
        out_specs=(VMEM, VMEM),
        compiler_params=params(),
    )(span)
    asked = swap(labels[:, None, :], 1)[:, 0, :]
    packed = pl.pallas_call(
        functools.partial(pack_kernel, devices, capacity),
        out_shape=shape_of((slots, WIDE), jnp.bfloat16),
        in_specs=[VMEM] * 8,
        out_specs=VMEM,
        scratch_shapes=[
            pltpu.VMEM((WIDE, columns), jnp.bfloat16),
            pltpu.VMEM((slots, columns), jnp.bfloat16),
        ],
        compiler_params=params(),
    )(
        asked, interp_index, interp_weight.reshape(4 * levels, columns), surface_source[None, :],
        cos_zenith[None, :], albedo[None, :], sunlit[None, :], sw_slot[None, :],
    )
    arrived = swap(packed.reshape(devices, capacity, WIDE), 2).reshape(slots, WIDE)
    g_lw, g_sw = table_lw.shape[0], table_sw.shape[0]
    sw_all = devices * (columns // 2)
    row_slots = (stripes * columns, stripes * (columns // 2))
    heating_lw, heating_sw, surface = pl.pallas_call(
        functools.partial(radiation_kernel, row_slots),
        out_shape=(
            shape_of((levels, columns), jnp.float32),
            shape_of((levels, columns), jnp.float32),
            shape_of((sw_all // LANES, LANES), jnp.float32),
        ),
        in_specs=[VMEM] * 10,
        out_specs=(VMEM,) * 3,
        scratch_shapes=[
            pltpu.VMEM((WIDE, columns), jnp.float32),
            pltpu.VMEM((levels, g_sw, WIDE), jnp.float32),
            pltpu.VMEM((levels, g_sw, WIDE), jnp.float32),
            pltpu.VMEM((levels, g_lw, WIDE), jnp.float32),
            pltpu.VMEM((levels, 8, WIDE), jnp.float32),
            pltpu.VMEM((levels, 8, WIDE), jnp.float32),
            pltpu.VMEM((1, columns), jnp.float32),
        ],
        compiler_params=params(),
    )(
        arrived, place, span, absorber_path, cloud_depth, planck_source, table_lw, table_sw,
        planck_frac[:, None], solar_weight[:, None],
    )
    sw_surface = collect(surface.reshape(devices, -1, LANES), 3)
    return heating_lw, heating_sw, sw_surface.reshape(columns // 2)


def solution(mesh):
    wide = P(None, AXES)
    flat = P(AXES)
    in_specs = (
        wide, wide, wide, flat, flat, wide, P(None, None, AXES), flat, flat, flat, flat,
        P(), P(), P(), P(),
    )
    out_specs = (wide, wide, flat)
    return jax.shard_map(body, mesh=mesh, in_specs=in_specs, out_specs=out_specs, check_vma=False)
```

```python
import functools
import math

import jax
import jax.numpy as jnp
from jax import lax
from jax.experimental import pallas as pl
from jax.experimental.pallas import tpu as pltpu
from jax.sharding import PartitionSpec as P

TEMPS = 14
PRESS = 64
LANES = 128
WIDE = 256
HALF = 64
DARK = 128
AXES = ("dyn", "col")
LOG2E = math.log2(math.e)
DIFFUSE = -1.66 * LOG2E
VMEM = pl.BlockSpec(memory_space=pltpu.VMEM)


def iota(shape, dim):
    return lax.broadcasted_iota(jnp.int32, shape, dim)


def hot(mask):
    return jnp.where(mask, 1.0, 0.0).astype(jnp.bfloat16)


def contract(a, b, dims):
    return lax.dot_general(a, b, (dims, ((), ())), preferred_element_type=jnp.float32)


def pieces(values):
    high = values.astype(jnp.bfloat16)
    rest = values - high.astype(jnp.float32)
    middle = rest.astype(jnp.bfloat16)
    low = (rest - middle.astype(jnp.float32)).astype(jnp.bfloat16)
    return high, middle, low


def whereabouts():
    stripes = lax.axis_size("col")
    devices = lax.axis_size("dyn") * stripes
    return lax.axis_index("dyn") * stripes + lax.axis_index("col"), stripes, devices


def peer(flat, stripes):
    return (flat // stripes, flat % stripes)


def call_out():
    me, stripes, devices = whereabouts()
    barrier = pltpu.get_barrier_semaphore()

    def signal(step, carry):
        pl.semaphore_signal(
            barrier, inc=1, device_id=peer((me + step) % devices, stripes),
            device_id_type=pl.DeviceIdType.MESH,
        )
        return carry

    lax.fori_loop(1, devices, signal, 0)


def hear_all():
    devices = whereabouts()[2]
    pl.semaphore_wait(pltpu.get_barrier_semaphore(), devices - 1)


def swap_blocks(pairs, own):
    me, stripes, devices = whereabouts()

    def copy_of(step, source, landing, send, receive):
        target = (me + step) % devices
        return pltpu.make_async_remote_copy(
            src_ref=source.at[target], dst_ref=landing.at[me],
            send_sem=send.at[step], recv_sem=receive.at[step],
            device_id=peer(target, stripes), device_id_type=pl.DeviceIdType.MESH,
        )

    def start(step, carry):
        for pair in pairs:
            copy_of(step, *pair).start()
        return carry

    def finish(step, carry):
        for pair in pairs:
            copy_of(step, *pair).wait()
        return carry

    kept = [
        pltpu.make_async_copy(pair[0].at[me], pair[1].at[me], own.at[at])
        for at, pair in enumerate(pairs)
    ]
    for copy in kept:
        copy.start()
    lax.fori_loop(1, devices, start, 0)
    for copy in kept:
        copy.wait()
    lax.fori_loop(1, devices, finish, 0)


def fold_rows(capacity):
    return max(16, capacity // 2)


def plan(span, devices, capacity):
    columns = span.shape[1]
    target = span >> (columns.bit_length() - 1)
    where = span & (columns - 1)
    marked = target == iota((devices, columns), 0)
    before = hot(iota((columns, columns), 0) < iota((columns, columns), 1))
    counts = contract(hot(marked), before, ((1,), (0,)))
    rank = jnp.sum(jnp.where(marked, counts, 0.0), axis=0, keepdims=True).astype(jnp.int32)
    ranked = hot(rank == iota((LANES, columns), 0))
    high = jnp.where(marked, ((where >> 5) + 1).astype(jnp.float32), 0.0).astype(jnp.bfloat16)
    low = jnp.where(marked, (where & 31).astype(jnp.float32), 0.0).astype(jnp.bfloat16)
    dims = ((1,), (1,))
    labels = contract(high, ranked, dims) * 32.0 + contract(low, ranked, dims) - 32.0
    return labels, target * capacity + rank


def exchange_kernel(
    devices, capacity, span_ref, index_ref, weight_ref, surface_ref, cosine_ref, albedo_ref,
    sunlit_ref, slot_ref, heavy_ref, light_ref, place_ref,
    rows, chosen, heavy_out, light_out, label_out, label_in,
    label_send, label_receive, heavy_send, heavy_receive, light_send, light_receive, own,
):
    levels, columns = index_ref.shape
    call_out()
    labels, place = plan(span_ref[...], devices, capacity)
    place_ref[...] = place
    label_out[...] = labels[:, None, :]
    index = index_ref[...]
    rows[0 : 4 * levels, :] = weight_ref[...]
    cell = ((index & (PRESS - 1)) + PRESS) << (index >> 6)
    slot = slot_ref[...]
    scalars = [
        *pieces(surface_ref[...]),
        *pieces(cosine_ref[...]),
        *pieces(albedo_ref[...]),
        jnp.where(sunlit_ref[...] == 1, slot >> 7, DARK).astype(jnp.float32).astype(jnp.bfloat16),
        (slot & (LANES - 1)).astype(jnp.float32).astype(jnp.bfloat16),
    ]
    scalars = [values.astype(jnp.float32) for values in scalars]
    blank = jnp.zeros((HALF - levels - len(scalars), columns), jnp.float32)
    others = jnp.concatenate([cell.astype(jnp.float32)] + scalars + [blank], axis=0)
    others = others.astype(jnp.bfloat16)
    rows[4 * levels : 4 * levels + HALF, :] = others
    rows[4 * levels + HALF :, :] = others
    hear_all()
    swap_blocks([(label_out, label_in, label_send, label_receive)], own)
    labels = label_in[...].reshape(devices, LANES)
    if devices < LANES:
        labels = jnp.concatenate(
            [labels, jnp.zeros((LANES - devices, LANES), jnp.float32)], axis=0
        )
    asked = jnp.transpose(labels).astype(jnp.int32)
    position = iota((capacity, columns), 1)
    for sender in range(devices):
        match = asked[0:capacity, sender : sender + 1] == position
        chosen[sender * capacity : (sender + 1) * capacity, :] = hot(match)
    packed = contract(chosen[...], rows[...], ((1,), (1,)))
    heavy_out[...] = packed[:, :LANES].reshape(devices, capacity, LANES).astype(jnp.bfloat16)
    folded = fold_rows(capacity)
    light = packed[:, LANES:].reshape(devices, capacity, LANES)
    if folded < capacity:
        left = iota((devices, folded, LANES), 2) < HALF
        light = jnp.where(left, light[:, :folded], light[:, folded:])
    light_out[...] = light.astype(jnp.bfloat16)
    swap_blocks(
        [
            (heavy_out, heavy_ref, heavy_send, heavy_receive),
            (light_out, light_ref, light_send, light_receive),
        ],
        own,
    )


def collect_kernel(source, total, landing, send, receive, own):
    call_out()
    hear_all()
    swap_blocks([(source, landing, send, receive)], own)
    total[...] = jnp.sum(landing[...], axis=0)


def collect(values, ident):
    devices = values.shape[0]
    return pl.pallas_call(
        collect_kernel,
        out_shape=shape_of(values.shape[1:], values.dtype),
        in_specs=[VMEM],
        out_specs=VMEM,
        scratch_shapes=[
            pltpu.VMEM(values.shape, values.dtype),
            pltpu.SemaphoreType.DMA((devices,)),
            pltpu.SemaphoreType.DMA((devices,)),
            pltpu.SemaphoreType.DMA((1,)),
        ],
        compiler_params=pltpu.CompilerParams(collective_id=ident, has_side_effects=True),
    )(values)


def radiation_kernel(
    row_slots, capacity, heavy_ref, light_ref, place_ref, span_ref, path_ref, cloud_ref,
    planck_ref, table_lw_ref, table_sw_ref, frac_ref, solar_ref, lw_ref, sw_ref, surface_ref,
    column_ref, beam_t, diffuse_t, long_t, lw_down, lw_up, sw_down, sw_up, ground_ref,
    solar_row, frac_lanes, solar_lanes, step_down, step_up,
):
    levels, columns = path_ref.shape
    g_lw, g_sw = table_lw_ref.shape[0], table_sw_ref.shape[0]
    place = place_ref[...]

    def pick(source, index):
        part = min(512, source.shape[0])
        total = None
        for start in range(0, source.shape[0], part):
            here = hot(index == iota((part, columns), 0) + start)
            term = contract(source[start : start + part, :], here, ((0,), (0,)))
            total = term if total is None else total + term
        return total

    heavy_rows = 4 * levels
    base = heavy_rows + levels
    press_base = heavy_rows + HALF
    column_ref[0:heavy_rows, :] = pick(heavy_ref, place)
    folded = fold_rows(capacity)
    sender = place >> (capacity.bit_length() - 1)
    rank = place & (capacity - 1)
    others = pick(light_ref, sender * folded + (rank & (folded - 1)))
    column_ref[heavy_rows:press_base, :] = jnp.where(
        rank < folded, others[:HALF], others[HALF:]
    )
    cell = column_ref[heavy_rows:base, :]
    temp = jnp.zeros_like(cell)
    shrink = jnp.ones_like(cell)
    for k in range(1, TEMPS):
        above = cell >= float(PRESS << k)
        temp = jnp.where(above, float(k), temp)
        shrink = jnp.where(above, 0.5**k, shrink)
    column_ref[heavy_rows:base, :] = temp
    column_ref[press_base : press_base + levels, :] = cell * shrink - float(PRESS)
    tile = WIDE
    table = jnp.concatenate([table_lw_ref[...], table_sw_ref[...]], axis=0)
    solar_row[...] = jnp.zeros_like(solar_row)
    solar_row[:, 0:g_sw] = solar_ref[...]
    frac_lanes[...] = jnp.transpose(jnp.broadcast_to(frac_ref[...], (LANES, g_lw)))
    solar_lanes[...] = jnp.transpose(jnp.broadcast_to(solar_row[...], (LANES, WIDE)))
    weight_sum = jnp.sum(frac_ref[...])
    solar_sum = jnp.sum(solar_ref[...])

    def scalar(offset, count, cols):
        values = column_ref[base + offset : base + offset + 1, cols]
        for piece in range(1, count):
            values = values + column_ref[base + offset + piece : base + offset + piece + 1, cols]
        return values

    def column_tile(step, carry):
        cols = pl.ds(pl.multiple_of(step * tile, tile), tile)
        surface = scalar(0, 3, cols)
        cosine = scalar(3, 3, cols)
        albedo = scalar(6, 3, cols)
        lit = scalar(9, 1, cols) < DARK
        slant = -LOG2E / cosine
        entry = iota((PRESS, tile), 0)

        def absorb_level(level, carry):
            def row(first):
                return column_ref[pl.ds(first + level, 1), cols]

            w0, w1, w2, w3 = (row(k * levels) for k in range(4))
            press = row(press_base).astype(jnp.int32)
            temp = row(4 * levels)
            offset = entry - press
            zero = jnp.zeros((), jnp.float32)
            near = jnp.where(offset == 0, w0, jnp.where(offset == 1, w1, zero))
            wrap = offset == 1 - PRESS
            far = jnp.where(
                offset == 0, w2, jnp.where(offset == 1, w3, jnp.where(wrap, w1, zero))
            )
            last = jnp.where(wrap[0:16], w3, zero).astype(jnp.bfloat16)
            near = near.astype(jnp.bfloat16)
            far = far.astype(jnp.bfloat16)
            temp = jnp.broadcast_to(temp.astype(jnp.bfloat16), (16, tile))
            hits = [temp == jnp.full((), k, jnp.bfloat16) for k in range(TEMPS)]
            blank = jnp.zeros((16, tile), jnp.bfloat16)
            blocks = []
            for k in range(TEMPS):
                for sub in range(0, PRESS, 16):
                    rest = blank
                    if k >= 2 and sub == 0:
                        rest = jnp.where(hits[k - 2], last, rest)
                    if k >= 1:
                        rest = jnp.where(hits[k - 1], far[sub : sub + 16], rest)
                    blocks.append(jnp.where(hits[k], near[sub : sub + 16], rest))
            mixing = jnp.concatenate(blocks, axis=0)
            absorb = jnp.dot(table, mixing, preferred_element_type=jnp.float32)
            path = path_ref[pl.ds(level, 1), cols]
            cloud = cloud_ref[pl.ds(level, 1), cols]
            long_t[level] = jnp.exp2(
                absorb[:g_lw] * (path * DIFFUSE) + cloud * DIFFUSE
            )
            beam_t[level] = jnp.exp2(absorb[g_lw:] * (path * slant) + cloud * slant)
            diffuse_t[level] = jnp.exp2(
                absorb[g_lw:] * (path * DIFFUSE) + cloud * DIFFUSE
            )
            return carry

        lax.fori_loop(0, levels, absorb_level, 0, unroll=4)

        for sums in (lw_down, lw_up, sw_down, sw_up):
            sums[...] = jnp.zeros_like(sums)
        planck = planck_ref[:, cols]
        level_gap = jnp.zeros((1, tile), jnp.float32)
        steps = planck[:-1] - planck[1:]
        step_down[...] = jnp.concatenate([-planck[:1], steps, level_gap], axis=0)[:, None, :]
        step_up[...] = jnp.concatenate(
            [level_gap, -steps, surface - planck[-1:]], axis=0
        )[:, None, :]
        quarter_lw, quarter_sw = g_lw // 4, g_sw // 4

        def fold(values):
            return jnp.sum(values.reshape(-1, 8, values.shape[-1]), axis=0)

        def fluxes(work, carry):
            quarter = work // 2
            half = work % 2
            lanes = pl.ds(pl.multiple_of(half * LANES, LANES), LANES)
            long_g = pl.ds(pl.multiple_of(quarter * quarter_lw, 8), quarter_lw)
            sun_g = pl.ds(pl.multiple_of(quarter * quarter_sw, 8), quarter_sw)
            frac = frac_lanes[long_g, :]

            def down(level, state):
                flux, beam = state
                passed = flux * long_t[level, long_g, lanes]
                beam = beam * beam_t[level, sun_g, lanes]
                lw_down[level, :, lanes] += fold(passed * frac)
                sw_down[level, :, lanes] += fold(beam)
                return passed + step_down[level + 1, :, lanes], beam

            flux = jnp.broadcast_to(step_down[0, :, lanes], (quarter_lw, LANES))
            flux, beam = lax.fori_loop(0, levels, down, (flux, solar_lanes[sun_g, :]), unroll=4)

            def up(back, state):
                flux, beam = state
                level = levels - 1 - back
                passed = flux * long_t[level, long_g, lanes]
                beam = beam * diffuse_t[level, sun_g, lanes]
                lw_up[level, :, lanes] += fold(passed * frac)
                sw_up[level, :, lanes] += fold(beam)
                return passed + step_up[level, :, lanes], beam

            flux = jnp.broadcast_to(step_up[levels, :, lanes], (quarter_lw, LANES))
            lax.fori_loop(0, levels, up, (flux, beam), unroll=4)
            return carry

        lax.fori_loop(0, 8, fluxes, 0)

        own = planck * weight_sum
        below = jnp.sum(lw_down[...], axis=1) + own
        above = jnp.sum(lw_up[...], axis=1) + own
        ground = surface * weight_sum
        entering_down = jnp.concatenate([jnp.zeros((1, tile), jnp.float32), below[:-1]], axis=0)
        entering_up = jnp.concatenate([above[1:], ground], axis=0)
        lw_ref[:, cols] = (entering_down - below) + (entering_up - above)

        beam = jnp.sum(sw_down[...], axis=1) * cosine
        reflect = albedo * cosine
        diffuse = jnp.sum(sw_up[...], axis=1) * reflect
        top = solar_sum * cosine
        arriving = jnp.concatenate([top, beam[:-1]], axis=0)
        rising = jnp.concatenate([diffuse[1:], albedo * beam[-1:]], axis=0)
        heat = (arriving - beam) + (rising - diffuse)
        sw_ref[:, cols] = jnp.where(lit, heat, 0.0)
        ground_ref[:, cols] = jnp.where(lit, (1.0 - albedo) * beam[-1:], 0.0)
        return carry

    lax.fori_loop(0, columns // tile, column_tile, 0)

    groups = surface_ref.shape[0]
    every = pl.ds(0, columns)
    slot_high = scalar(9, 1, every).astype(jnp.int32)
    slot_low = scalar(10, 1, every).astype(jnp.int32)
    dyn_row = span_ref[...] // row_slots[0]
    home = dyn_row * (row_slots[1] // LANES) + slot_high
    at_home = home == iota((groups, columns), 0)
    at_lane = hot(slot_low == iota((LANES, columns), 0))
    total = None
    for piece in pieces(ground_ref[...]):
        spread = jnp.where(at_home, piece.astype(jnp.float32), 0.0).astype(jnp.bfloat16)
        term = contract(spread, at_lane, ((1,), (1,)))
        total = term if total is None else total + term
    surface_ref[...] = total


def params(**more):
    return pltpu.CompilerParams(vmem_limit_bytes=56 * 1024 * 1024, **more)


def shape_of(shape, dtype):
    return jax.ShapeDtypeStruct(shape, dtype)


def body(
    planck_source, absorber_path, cloud_depth, span_map, surface_source, interp_index,
    interp_weight, sunlit, sw_slot, cos_zenith, albedo, table_lw, table_sw, planck_frac,
    solar_weight,
):
    levels, columns = planck_source.shape
    stripes = lax.axis_size("col")
    devices = lax.axis_size("dyn") * stripes
    capacity = 2 * columns // devices
    slots = devices * capacity
    span = span_map[None, :]
    folded = fold_rows(capacity)
    link = pltpu.SemaphoreType.DMA((devices,))
    place_anywhere = pl.BlockSpec(memory_space=pl.ANY)
    heavy, light, place = pl.pallas_call(
        functools.partial(exchange_kernel, devices, capacity),
        out_shape=(
            shape_of((devices, capacity, LANES), jnp.bfloat16),
            shape_of((devices, folded, LANES), jnp.bfloat16),
            shape_of((1, columns), jnp.int32),
        ),
        in_specs=[VMEM] * 8,
        out_specs=(place_anywhere, place_anywhere, VMEM),
        scratch_shapes=[
            pltpu.VMEM((WIDE, columns), jnp.bfloat16),
            pltpu.VMEM((slots, columns), jnp.bfloat16),
            pltpu.VMEM((devices, capacity, LANES), jnp.bfloat16),
            pltpu.VMEM((devices, folded, LANES), jnp.bfloat16),
            pltpu.VMEM((devices, 1, LANES), jnp.float32),
            pltpu.VMEM((devices, 1, LANES), jnp.float32),
            *[link] * 6,
            pltpu.SemaphoreType.DMA((2,)),
        ],
        compiler_params=params(collective_id=1, has_side_effects=True),
    )(
        span, interp_index, interp_weight.reshape(4 * levels, columns), surface_source[None, :],
        cos_zenith[None, :], albedo[None, :], sunlit[None, :], sw_slot[None, :],
    )
    g_lw, g_sw = table_lw.shape[0], table_sw.shape[0]
    sw_all = devices * (columns // 2)
    row_slots = (stripes * columns, stripes * (columns // 2))
    heating_lw, heating_sw, surface = pl.pallas_call(
        functools.partial(radiation_kernel, row_slots, capacity),
        out_shape=(
            shape_of((levels, columns), jnp.float32),
            shape_of((levels, columns), jnp.float32),
            shape_of((sw_all // LANES, LANES), jnp.float32),
        ),
        in_specs=[VMEM] * 11,
        out_specs=(VMEM,) * 3,
        scratch_shapes=[
            pltpu.VMEM((WIDE, columns), jnp.float32),
            pltpu.VMEM((levels, g_sw, WIDE), jnp.float32),
            pltpu.VMEM((levels, g_sw, WIDE), jnp.float32),
            pltpu.VMEM((levels, g_lw, WIDE), jnp.float32),
            *[pltpu.VMEM((levels, 8, WIDE), jnp.float32)] * 4,
            pltpu.VMEM((1, columns), jnp.float32),
            pltpu.VMEM((1, WIDE), jnp.float32),
            pltpu.VMEM((g_lw, LANES), jnp.float32),
            pltpu.VMEM((WIDE, LANES), jnp.float32),
            *[pltpu.VMEM((levels + 1, 1, WIDE), jnp.float32)] * 2,
        ],
        compiler_params=params(),
    )(
        heavy.reshape(slots, LANES), light.reshape(devices * folded, LANES), place, span, absorber_path, cloud_depth, planck_source, table_lw, table_sw,
        planck_frac[None, :], solar_weight[None, :],
    )
    sw_surface = collect(surface.reshape(devices, -1, LANES), 2)
    return heating_lw, heating_sw, sw_surface.reshape(columns // 2)


def solution(mesh):
    wide = P(None, AXES)
    flat = P(AXES)
    in_specs = (
        wide, wide, wide, flat, flat, wide, P(None, None, AXES), flat, flat, flat, flat,
        P(), P(), P(), P(),
    )
    out_specs = (wide, wide, flat)
    return jax.shard_map(body, mesh=mesh, in_specs=in_specs, out_specs=out_specs, check_vma=False)
```

```python
import functools
import math

import jax
import jax.numpy as jnp
from jax import lax
from jax.experimental import pallas as pl
from jax.experimental.pallas import tpu as pltpu
from jax.sharding import PartitionSpec as P

TEMPS = 14
PRESS = 64
LANES = 128
WIDE = 256
HALF = 64
DARK = 128
AXES = ("dyn", "col")
LOG2E = math.log2(math.e)
DIFFUSE = -1.66 * LOG2E
VMEM = pl.BlockSpec(memory_space=pltpu.VMEM)


def iota(shape, dim):
    return lax.broadcasted_iota(jnp.int32, shape, dim)


def hot(mask):
    return jnp.where(mask, 1.0, 0.0).astype(jnp.bfloat16)


def contract(a, b, dims):
    return lax.dot_general(a, b, (dims, ((), ())), preferred_element_type=jnp.float32)


def pieces(values):
    high = values.astype(jnp.bfloat16)
    rest = values - high.astype(jnp.float32)
    middle = rest.astype(jnp.bfloat16)
    low = (rest - middle.astype(jnp.float32)).astype(jnp.bfloat16)
    return high, middle, low


def whereabouts():
    stripes = lax.axis_size("col")
    devices = lax.axis_size("dyn") * stripes
    return lax.axis_index("dyn") * stripes + lax.axis_index("col"), stripes, devices


def peer(flat, stripes):
    return (flat // stripes, flat % stripes)


def call_out():
    me, stripes, devices = whereabouts()
    barrier = pltpu.get_barrier_semaphore()

    def signal(step, carry):
        pl.semaphore_signal(
            barrier, inc=1, device_id=peer((me + step) % devices, stripes),
            device_id_type=pl.DeviceIdType.MESH,
        )
        return carry

    lax.fori_loop(1, devices, signal, 0)


def hear_all():
    devices = whereabouts()[2]
    pl.semaphore_wait(pltpu.get_barrier_semaphore(), devices - 1)


def swap_blocks(pairs, own):
    me, stripes, devices = whereabouts()

    def copy_of(step, source, landing, send, receive):
        target = (me + step) % devices
        return pltpu.make_async_remote_copy(
            src_ref=source.at[target], dst_ref=landing.at[me],
            send_sem=send.at[step], recv_sem=receive.at[step],
            device_id=peer(target, stripes), device_id_type=pl.DeviceIdType.MESH,
        )

    def start(step, carry):
        for pair in pairs:
            copy_of(step, *pair).start()
        return carry

    def finish(step, carry):
        for pair in pairs:
            copy_of(step, *pair).wait()
        return carry

    kept = [
        pltpu.make_async_copy(pair[0].at[me], pair[1].at[me], own.at[at])
        for at, pair in enumerate(pairs)
    ]
    for copy in kept:
        copy.start()
    lax.fori_loop(1, devices, start, 0)
    for copy in kept:
        copy.wait()
    lax.fori_loop(1, devices, finish, 0)


def fold_rows(capacity):
    return max(16, capacity // 2)


def plan(span, devices, capacity):
    columns = span.shape[1]
    target = span >> (columns.bit_length() - 1)
    where = span & (columns - 1)
    marked = target == iota((devices, columns), 0)
    before = hot(iota((columns, columns), 0) < iota((columns, columns), 1))
    counts = contract(hot(marked), before, ((1,), (0,)))
    rank = jnp.sum(jnp.where(marked, counts, 0.0), axis=0, keepdims=True).astype(jnp.int32)
    ranked = hot(rank == iota((LANES, columns), 0))
    high = jnp.where(marked, ((where >> 5) + 1).astype(jnp.float32), 0.0).astype(jnp.bfloat16)
    low = jnp.where(marked, (where & 31).astype(jnp.float32), 0.0).astype(jnp.bfloat16)
    dims = ((1,), (1,))
    labels = contract(high, ranked, dims) * 32.0 + contract(low, ranked, dims) - 32.0
    return labels, target * capacity + rank


def exchange_kernel(
    devices, capacity, span_ref, index_ref, weight_ref, surface_ref, cosine_ref, albedo_ref,
    sunlit_ref, slot_ref, heavy_ref, light_ref, place_ref,
    rows, chosen, heavy_out, light_out, label_out, label_in,
    label_send, label_receive, heavy_send, heavy_receive, light_send, light_receive, own,
):
    levels, columns = index_ref.shape
    call_out()
    labels, place = plan(span_ref[...], devices, capacity)
    place_ref[...] = place
    label_out[...] = labels[:, None, :]
    index = index_ref[...]
    rows[0 : 4 * levels, :] = weight_ref[...]
    cell = ((index & (PRESS - 1)) + PRESS) << (index >> 6)
    slot = slot_ref[...]
    scalars = [
        *pieces(surface_ref[...]),
        *pieces(cosine_ref[...]),
        *pieces(albedo_ref[...]),
        jnp.where(sunlit_ref[...] == 1, slot >> 7, DARK).astype(jnp.float32).astype(jnp.bfloat16),
        (slot & (LANES - 1)).astype(jnp.float32).astype(jnp.bfloat16),
    ]
    scalars = [values.astype(jnp.float32) for values in scalars]
    blank = jnp.zeros((HALF - levels - len(scalars), columns), jnp.float32)
    others = jnp.concatenate([cell.astype(jnp.float32)] + scalars + [blank], axis=0)
    others = others.astype(jnp.bfloat16)
    rows[4 * levels : 4 * levels + HALF, :] = others
    rows[4 * levels + HALF :, :] = others
    hear_all()
    swap_blocks([(label_out, label_in, label_send, label_receive)], own)
    labels = label_in[...].reshape(devices, LANES)
    if devices < LANES:
        labels = jnp.concatenate(
            [labels, jnp.zeros((LANES - devices, LANES), jnp.float32)], axis=0
        )
    asked = jnp.transpose(labels).astype(jnp.int32)
    position = iota((capacity, columns), 1)
    for sender in range(devices):
        match = asked[0:capacity, sender : sender + 1] == position
        chosen[sender * capacity : (sender + 1) * capacity, :] = hot(match)
    packed = contract(chosen[...], rows[...], ((1,), (1,)))
    heavy_out[...] = packed[:, :LANES].reshape(devices, capacity, LANES).astype(jnp.bfloat16)
    folded = fold_rows(capacity)
    light = packed[:, LANES:].reshape(devices, capacity, LANES)
    if folded < capacity:
        left = iota((devices, folded, LANES), 2) < HALF
        light = jnp.where(left, light[:, :folded], light[:, folded:])
    light_out[...] = light.astype(jnp.bfloat16)
    swap_blocks(
        [
            (heavy_out, heavy_ref, heavy_send, heavy_receive),
            (light_out, light_ref, light_send, light_receive),
        ],
        own,
    )


def collect_kernel(source, total, landing, send, receive, own):
    call_out()
    hear_all()
    swap_blocks([(source, landing, send, receive)], own)
    total[...] = jnp.sum(landing[...], axis=0)


def collect(values, ident):
    devices = values.shape[0]
    return pl.pallas_call(
        collect_kernel,
        out_shape=shape_of(values.shape[1:], values.dtype),
        in_specs=[VMEM],
        out_specs=VMEM,
        scratch_shapes=[
            pltpu.VMEM(values.shape, values.dtype),
            pltpu.SemaphoreType.DMA((devices,)),
            pltpu.SemaphoreType.DMA((devices,)),
            pltpu.SemaphoreType.DMA((1,)),
        ],
        compiler_params=pltpu.CompilerParams(collective_id=ident, has_side_effects=True),
    )(values)


def radiation_kernel(
    row_slots, capacity, heavy_ref, light_ref, place_ref, span_ref, path_ref, cloud_ref,
    planck_ref, table_lw_ref, table_sw_ref, frac_ref, solar_ref, lw_ref, sw_ref, surface_ref,
    column_ref, flux_ref, beam_ref, diffuse_t, long_t, lw_down, lw_up, sw_down, sw_up, ground_ref,
    solar_row, frac_lanes, solar_lanes, step_down, step_up,
):
    levels, columns = path_ref.shape
    g_lw, g_sw = table_lw_ref.shape[0], table_sw_ref.shape[0]
    place = place_ref[...]

    def pick(source, index):
        part = min(512, source.shape[0])
        total = None
        for start in range(0, source.shape[0], part):
            here = hot(index == iota((part, columns), 0) + start)
            term = contract(source[start : start + part, :], here, ((0,), (0,)))
            total = term if total is None else total + term
        return total

    heavy_rows = 4 * levels
    base = heavy_rows + levels
    press_base = heavy_rows + HALF
    column_ref[0:heavy_rows, :] = pick(heavy_ref, place)
    folded = fold_rows(capacity)
    sender = place >> (capacity.bit_length() - 1)
    rank = place & (capacity - 1)
    others = pick(light_ref, sender * folded + (rank & (folded - 1)))
    column_ref[heavy_rows:press_base, :] = jnp.where(
        rank < folded, others[:HALF], others[HALF:]
    )
    cell = column_ref[heavy_rows:base, :]
    temp = jnp.zeros_like(cell)
    shrink = jnp.ones_like(cell)
    for k in range(1, TEMPS):
        above = cell >= float(PRESS << k)
        temp = jnp.where(above, float(k), temp)
        shrink = jnp.where(above, 0.5**k, shrink)
    column_ref[heavy_rows:base, :] = temp
    column_ref[press_base : press_base + levels, :] = cell * shrink - float(PRESS)
    tile = WIDE
    table = jnp.concatenate([table_lw_ref[...], table_sw_ref[...]], axis=0)
    solar_row[...] = jnp.zeros_like(solar_row)
    solar_row[:, 0:g_sw] = solar_ref[...]
    frac_lanes[...] = jnp.transpose(jnp.broadcast_to(frac_ref[...], (LANES, g_lw)))
    solar_lanes[...] = jnp.transpose(jnp.broadcast_to(solar_row[...], (LANES, WIDE)))
    weight_sum = jnp.sum(frac_ref[...])
    solar_sum = jnp.sum(solar_ref[...])

    def scalar(offset, count, cols):
        values = column_ref[base + offset : base + offset + 1, cols]
        for piece in range(1, count):
            values = values + column_ref[base + offset + piece : base + offset + piece + 1, cols]
        return values

    def column_tile(step, carry):
        cols = pl.ds(pl.multiple_of(step * tile, tile), tile)
        surface = scalar(0, 3, cols)
        cosine = scalar(3, 3, cols)
        albedo = scalar(6, 3, cols)
        lit = scalar(9, 1, cols) < DARK
        slant = -LOG2E / cosine
        entry = iota((PRESS, tile), 0)

        planck = planck_ref[:, cols]
        level_gap = jnp.zeros((1, tile), jnp.float32)
        steps = planck[:-1] - planck[1:]
        step_down[...] = jnp.concatenate([-planck[:1], steps, level_gap], axis=0)[:, None, :]
        step_up[...] = jnp.concatenate(
            [level_gap, -steps, surface - planck[-1:]], axis=0
        )[:, None, :]
        flux_ref[...] = jnp.broadcast_to(step_down[0], (g_lw, tile))
        beam_ref[...] = jnp.concatenate([solar_lanes[0:g_sw, :]] * 2, axis=1)

        def fold(values):
            return jnp.sum(values.reshape(-1, 8, values.shape[-1]), axis=0)

        def absorb_level(level, carry):
            frac = jnp.concatenate([frac_lanes[...]] * 2, axis=1)

            def row(first):
                return column_ref[pl.ds(first + level, 1), cols]

            w0, w1, w2, w3 = (row(k * levels) for k in range(4))
            press = row(press_base).astype(jnp.int32)
            temp = row(4 * levels)
            offset = entry - press
            zero = jnp.zeros((), jnp.float32)
            near = jnp.where(offset == 0, w0, jnp.where(offset == 1, w1, zero))
            wrap = offset == 1 - PRESS
            far = jnp.where(
                offset == 0, w2, jnp.where(offset == 1, w3, jnp.where(wrap, w1, zero))
            )
            last = jnp.where(wrap[0:16], w3, zero).astype(jnp.bfloat16)
            near = near.astype(jnp.bfloat16)
            far = far.astype(jnp.bfloat16)
            temp = jnp.broadcast_to(temp.astype(jnp.bfloat16), (16, tile))
            hits = [temp == jnp.full((), k, jnp.bfloat16) for k in range(TEMPS)]
            blank = jnp.zeros((16, tile), jnp.bfloat16)
            blocks = []
            for k in range(TEMPS):
                for sub in range(0, PRESS, 16):
                    rest = blank
                    if k >= 2 and sub == 0:
                        rest = jnp.where(hits[k - 2], last, rest)
                    if k >= 1:
                        rest = jnp.where(hits[k - 1], far[sub : sub + 16], rest)
                    blocks.append(jnp.where(hits[k], near[sub : sub + 16], rest))
            mixing = jnp.concatenate(blocks, axis=0)
            absorb = jnp.dot(table, mixing, preferred_element_type=jnp.float32)
            path = path_ref[pl.ds(level, 1), cols]
            cloud = cloud_ref[pl.ds(level, 1), cols]
            transmit = jnp.exp2(absorb[:g_lw] * (path * DIFFUSE) + cloud * DIFFUSE)
            long_t[level] = transmit
            passed = flux_ref[...] * transmit
            lw_down[level] = fold(passed * frac)
            flux_ref[...] = passed + step_down[level + 1]
            beam = beam_ref[...] * jnp.exp2(absorb[g_lw:] * (path * slant) + cloud * slant)
            sw_down[level] = fold(beam)
            beam_ref[...] = beam
            diffuse_t[level] = jnp.exp2(
                absorb[g_lw:] * (path * DIFFUSE) + cloud * DIFFUSE
            )
            return carry

        lax.fori_loop(0, levels, absorb_level, 0, unroll=4)

        for sums in (lw_up, sw_up):
            sums[...] = jnp.zeros_like(sums)
        quarter_lw, quarter_sw = g_lw // 4, g_sw // 4

        def fluxes(work, carry):
            quarter = work // 2
            half = work % 2
            lanes = pl.ds(pl.multiple_of(half * LANES, LANES), LANES)
            long_g = pl.ds(pl.multiple_of(quarter * quarter_lw, 8), quarter_lw)
            sun_g = pl.ds(pl.multiple_of(quarter * quarter_sw, 8), quarter_sw)
            frac = frac_lanes[long_g, :]

            def up(back, state):
                flux, beam = state
                level = levels - 1 - back
                passed = flux * long_t[level, long_g, lanes]
                beam = beam * diffuse_t[level, sun_g, lanes]
                lw_up[level, :, lanes] += fold(passed * frac)
                sw_up[level, :, lanes] += fold(beam)
                return passed + step_up[level, :, lanes], beam

            flux = jnp.broadcast_to(step_up[levels, :, lanes], (quarter_lw, LANES))
            lax.fori_loop(0, levels, up, (flux, beam_ref[sun_g, lanes]), unroll=4)
            return carry

        lax.fori_loop(0, 8, fluxes, 0)

        own = planck * weight_sum
        below = jnp.sum(lw_down[...], axis=1) + own
        above = jnp.sum(lw_up[...], axis=1) + own
        ground = surface * weight_sum
        entering_down = jnp.concatenate([jnp.zeros((1, tile), jnp.float32), below[:-1]], axis=0)
        entering_up = jnp.concatenate([above[1:], ground], axis=0)
        lw_ref[:, cols] = (entering_down - below) + (entering_up - above)

        beam = jnp.sum(sw_down[...], axis=1) * cosine
        reflect = albedo * cosine
        diffuse = jnp.sum(sw_up[...], axis=1) * reflect
        top = solar_sum * cosine
        arriving = jnp.concatenate([top, beam[:-1]], axis=0)
        rising = jnp.concatenate([diffuse[1:], albedo * beam[-1:]], axis=0)
        heat = (arriving - beam) + (rising - diffuse)
        sw_ref[:, cols] = jnp.where(lit, heat, 0.0)
        ground_ref[:, cols] = jnp.where(lit, (1.0 - albedo) * beam[-1:], 0.0)
        return carry

    lax.fori_loop(0, columns // tile, column_tile, 0)

    groups = surface_ref.shape[0]
    every = pl.ds(0, columns)
    slot_high = scalar(9, 1, every).astype(jnp.int32)
    slot_low = scalar(10, 1, every).astype(jnp.int32)
    dyn_row = span_ref[...] // row_slots[0]
    home = dyn_row * (row_slots[1] // LANES) + slot_high
    at_home = home == iota((groups, columns), 0)
    at_lane = hot(slot_low == iota((LANES, columns), 0))
    total = None
    for piece in pieces(ground_ref[...]):
        spread = jnp.where(at_home, piece.astype(jnp.float32), 0.0).astype(jnp.bfloat16)
        term = contract(spread, at_lane, ((1,), (1,)))
        total = term if total is None else total + term
    surface_ref[...] = total


def params(**more):
    return pltpu.CompilerParams(vmem_limit_bytes=56 * 1024 * 1024, **more)


def shape_of(shape, dtype):
    return jax.ShapeDtypeStruct(shape, dtype)


def body(
    planck_source, absorber_path, cloud_depth, span_map, surface_source, interp_index,
    interp_weight, sunlit, sw_slot, cos_zenith, albedo, table_lw, table_sw, planck_frac,
    solar_weight,
):
    levels, columns = planck_source.shape
    stripes = lax.axis_size("col")
    devices = lax.axis_size("dyn") * stripes
    capacity = 2 * columns // devices
    slots = devices * capacity
    span = span_map[None, :]
    folded = fold_rows(capacity)
    link = pltpu.SemaphoreType.DMA((devices,))
    place_anywhere = pl.BlockSpec(memory_space=pl.ANY)
    heavy, light, place = pl.pallas_call(
        functools.partial(exchange_kernel, devices, capacity),
        out_shape=(
            shape_of((devices, capacity, LANES), jnp.bfloat16),
            shape_of((devices, folded, LANES), jnp.bfloat16),
            shape_of((1, columns), jnp.int32),
        ),
        in_specs=[VMEM] * 8,
        out_specs=(place_anywhere, place_anywhere, VMEM),
        scratch_shapes=[
            pltpu.VMEM((WIDE, columns), jnp.bfloat16),
            pltpu.VMEM((slots, columns), jnp.bfloat16),
            pltpu.VMEM((devices, capacity, LANES), jnp.bfloat16),
            pltpu.VMEM((devices, folded, LANES), jnp.bfloat16),
            pltpu.VMEM((devices, 1, LANES), jnp.float32),
            pltpu.VMEM((devices, 1, LANES), jnp.float32),
            *[link] * 6,
            pltpu.SemaphoreType.DMA((2,)),
        ],
        compiler_params=params(collective_id=1, has_side_effects=True),
    )(
        span, interp_index, interp_weight.reshape(4 * levels, columns), surface_source[None, :],
        cos_zenith[None, :], albedo[None, :], sunlit[None, :], sw_slot[None, :],
    )
    g_lw, g_sw = table_lw.shape[0], table_sw.shape[0]
    sw_all = devices * (columns // 2)
    row_slots = (stripes * columns, stripes * (columns // 2))
    heating_lw, heating_sw, surface = pl.pallas_call(
        functools.partial(radiation_kernel, row_slots, capacity),
        out_shape=(
            shape_of((levels, columns), jnp.float32),
            shape_of((levels, columns), jnp.float32),
            shape_of((sw_all // LANES, LANES), jnp.float32),
        ),
        in_specs=[VMEM] * 11,
        out_specs=(VMEM,) * 3,
        scratch_shapes=[
            pltpu.VMEM((WIDE, columns), jnp.float32),
            pltpu.VMEM((g_lw, WIDE), jnp.float32),
            pltpu.VMEM((g_sw, WIDE), jnp.float32),
            pltpu.VMEM((levels, g_sw, WIDE), jnp.float32),
            pltpu.VMEM((levels, g_lw, WIDE), jnp.float32),
            *[pltpu.VMEM((levels, 8, WIDE), jnp.float32)] * 4,
            pltpu.VMEM((1, columns), jnp.float32),
            pltpu.VMEM((1, WIDE), jnp.float32),
            pltpu.VMEM((g_lw, LANES), jnp.float32),
            pltpu.VMEM((WIDE, LANES), jnp.float32),
            *[pltpu.VMEM((levels + 1, 1, WIDE), jnp.float32)] * 2,
        ],
        compiler_params=params(),
    )(
        heavy.reshape(slots, LANES), light.reshape(devices * folded, LANES), place, span, absorber_path, cloud_depth, planck_source, table_lw, table_sw,
        planck_frac[None, :], solar_weight[None, :],
    )
    sw_surface = collect(surface.reshape(devices, -1, LANES), 2)
    return heating_lw, heating_sw, sw_surface.reshape(columns // 2)


def solution(mesh):
    wide = P(None, AXES)
    flat = P(AXES)
    in_specs = (
        wide, wide, wide, flat, flat, wide, P(None, None, AXES), flat, flat, flat, flat,
        P(), P(), P(), P(),
    )
    out_specs = (wide, wide, flat)
    return jax.shard_map(body, mesh=mesh, in_specs=in_specs, out_specs=out_specs, check_vma=False)
```

```python
import functools
import math

import jax
import jax.numpy as jnp
from jax import lax
from jax.experimental import pallas as pl
from jax.experimental.pallas import tpu as pltpu
from jax.sharding import PartitionSpec as P

TEMPS = 14
PRESS = 64
LANES = 128
WIDE = 256
HALF = 64
DARK = 128
AXES = ("dyn", "col")
LOG2E = math.log2(math.e)
DIFFUSE = -1.66 * LOG2E
VMEM = pl.BlockSpec(memory_space=pltpu.VMEM)


def iota(shape, dim):
    return lax.broadcasted_iota(jnp.int32, shape, dim)


def hot(mask):
    return jnp.where(mask, 1.0, 0.0).astype(jnp.bfloat16)


def contract(a, b, dims):
    return lax.dot_general(a, b, (dims, ((), ())), preferred_element_type=jnp.float32)


def pieces(values):
    high = values.astype(jnp.bfloat16)
    rest = values - high.astype(jnp.float32)
    middle = rest.astype(jnp.bfloat16)
    low = (rest - middle.astype(jnp.float32)).astype(jnp.bfloat16)
    return high, middle, low


def whereabouts():
    stripes = lax.axis_size("col")
    devices = lax.axis_size("dyn") * stripes
    return lax.axis_index("dyn") * stripes + lax.axis_index("col"), stripes, devices


def peer(flat, stripes):
    return (flat // stripes, flat % stripes)


def call_out():
    me, stripes, devices = whereabouts()
    barrier = pltpu.get_barrier_semaphore()

    def signal(step, carry):
        pl.semaphore_signal(
            barrier, inc=1, device_id=peer((me + step) % devices, stripes),
            device_id_type=pl.DeviceIdType.MESH,
        )
        return carry

    lax.fori_loop(1, devices, signal, 0)


def hear_all():
    devices = whereabouts()[2]
    pl.semaphore_wait(pltpu.get_barrier_semaphore(), devices - 1)


def swap_blocks(pairs, own):
    me, stripes, devices = whereabouts()

    def copy_of(step, source, landing, send, receive):
        target = (me + step) % devices
        return pltpu.make_async_remote_copy(
            src_ref=source.at[target], dst_ref=landing.at[me],
            send_sem=send.at[step], recv_sem=receive.at[step],
            device_id=peer(target, stripes), device_id_type=pl.DeviceIdType.MESH,
        )

    def start(step, carry):
        for pair in pairs:
            copy_of(step, *pair).start()
        return carry

    def finish(step, carry):
        for pair in pairs:
            copy_of(step, *pair).wait()
        return carry

    kept = [
        pltpu.make_async_copy(pair[0].at[me], pair[1].at[me], own.at[at])
        for at, pair in enumerate(pairs)
    ]
    for copy in kept:
        copy.start()
    lax.fori_loop(1, devices, start, 0)
    for copy in kept:
        copy.wait()
    lax.fori_loop(1, devices, finish, 0)


def fold_rows(capacity):
    return max(16, capacity // 2)


def plan(span, devices, capacity):
    columns = span.shape[1]
    target = span >> (columns.bit_length() - 1)
    where = span & (columns - 1)
    marked = target == iota((devices, columns), 0)
    before = hot(iota((columns, columns), 0) < iota((columns, columns), 1))
    counts = contract(hot(marked), before, ((1,), (0,)))
    rank = jnp.sum(jnp.where(marked, counts, 0.0), axis=0, keepdims=True).astype(jnp.int32)
    ranked = hot(rank == iota((LANES, columns), 0))
    high = jnp.where(marked, ((where >> 5) + 1).astype(jnp.float32), 0.0).astype(jnp.bfloat16)
    low = jnp.where(marked, (where & 31).astype(jnp.float32), 0.0).astype(jnp.bfloat16)
    dims = ((1,), (1,))
    labels = contract(high, ranked, dims) * 32.0 + contract(low, ranked, dims) - 32.0
    return labels, target * capacity + rank


def exchange_kernel(
    devices, capacity, span_ref, index_ref, weight_ref, surface_ref, cosine_ref, albedo_ref,
    sunlit_ref, slot_ref, heavy_ref, light_ref, place_ref,
    rows, chosen, heavy_out, light_out, label_out, label_in,
    label_send, label_receive, heavy_send, heavy_receive, light_send, light_receive, own,
):
    levels, columns = index_ref.shape
    call_out()
    labels, place = plan(span_ref[...], devices, capacity)
    place_ref[...] = place
    label_out[...] = labels[:, None, :]
    index = index_ref[...]
    rows[0 : 4 * levels, :] = weight_ref[...]
    cell = ((index & (PRESS - 1)) + PRESS) << (index >> 6)
    slot = slot_ref[...]
    scalars = [
        *pieces(surface_ref[...]),
        *pieces(cosine_ref[...]),
        *pieces(albedo_ref[...]),
        jnp.where(sunlit_ref[...] == 1, slot >> 7, DARK).astype(jnp.float32).astype(jnp.bfloat16),
        (slot & (LANES - 1)).astype(jnp.float32).astype(jnp.bfloat16),
    ]
    scalars = [values.astype(jnp.float32) for values in scalars]
    blank = jnp.zeros((HALF - levels - len(scalars), columns), jnp.float32)
    others = jnp.concatenate([cell.astype(jnp.float32)] + scalars + [blank], axis=0)
    others = others.astype(jnp.bfloat16)
    rows[4 * levels : 4 * levels + HALF, :] = others
    rows[4 * levels + HALF :, :] = others
    hear_all()
    swap_blocks([(label_out, label_in, label_send, label_receive)], own)
    labels = label_in[...].reshape(devices, LANES)
    if devices < LANES:
        labels = jnp.concatenate(
            [labels, jnp.zeros((LANES - devices, LANES), jnp.float32)], axis=0
        )
    asked = jnp.transpose(labels).astype(jnp.int32)
    position = iota((capacity, columns), 1)
    for sender in range(devices):
        match = asked[0:capacity, sender : sender + 1] == position
        chosen[sender * capacity : (sender + 1) * capacity, :] = hot(match)
    packed = contract(chosen[...], rows[...], ((1,), (1,)))
    heavy_out[...] = packed[:, :LANES].reshape(devices, capacity, LANES).astype(jnp.bfloat16)
    folded = fold_rows(capacity)
    light = packed[:, LANES:].reshape(devices, capacity, LANES)
    if folded < capacity:
        left = iota((devices, folded, LANES), 2) < HALF
        light = jnp.where(left, light[:, :folded], light[:, folded:])
    light_out[...] = light.astype(jnp.bfloat16)
    swap_blocks(
        [
            (heavy_out, heavy_ref, heavy_send, heavy_receive),
            (light_out, light_ref, light_send, light_receive),
        ],
        own,
    )


def collect_kernel(source, total, landing, send, receive, own):
    call_out()
    hear_all()
    swap_blocks([(source, landing, send, receive)], own)
    total[...] = jnp.sum(landing[...], axis=0)


def collect(values, ident):
    devices = values.shape[0]
    return pl.pallas_call(
        collect_kernel,
        out_shape=shape_of(values.shape[1:], values.dtype),
        in_specs=[VMEM],
        out_specs=VMEM,
        scratch_shapes=[
            pltpu.VMEM(values.shape, values.dtype),
            pltpu.SemaphoreType.DMA((devices,)),
            pltpu.SemaphoreType.DMA((devices,)),
            pltpu.SemaphoreType.DMA((1,)),
        ],
        compiler_params=pltpu.CompilerParams(collective_id=ident, has_side_effects=True),
    )(values)


def radiation_kernel(
    row_slots, capacity, heavy_ref, light_ref, place_ref, span_ref, path_ref, cloud_ref,
    planck_ref, table_lw_ref, table_sw_ref, frac_ref, solar_ref, lw_ref, sw_ref, surface_ref,
    column_ref, flux_ref, beam_ref, diffuse_t, long_t, lw_down, lw_up, sw_down, sw_up, ground_ref,
    solar_row, frac_lanes, solar_lanes, step_down, step_up,
):
    levels, columns = path_ref.shape
    g_lw, g_sw = table_lw_ref.shape[0], table_sw_ref.shape[0]
    place = place_ref[...]

    def pick(source, index):
        part = min(512, source.shape[0])
        total = None
        for start in range(0, source.shape[0], part):
            here = hot(index == iota((part, columns), 0) + start)
            term = contract(source[start : start + part, :], here, ((0,), (0,)))
            total = term if total is None else total + term
        return total

    heavy_rows = 4 * levels
    base = heavy_rows + levels
    press_base = heavy_rows + HALF
    column_ref[0:heavy_rows, :] = pick(heavy_ref, place)
    folded = fold_rows(capacity)
    sender = place >> (capacity.bit_length() - 1)
    rank = place & (capacity - 1)
    others = pick(light_ref, sender * folded + (rank & (folded - 1)))
    column_ref[heavy_rows:press_base, :] = jnp.where(
        rank < folded, others[:HALF], others[HALF:]
    )
    cell = column_ref[heavy_rows:base, :]
    temp = jnp.zeros_like(cell)
    shrink = jnp.ones_like(cell)
    for k in range(1, TEMPS):
        above = cell >= float(PRESS << k)
        temp = jnp.where(above, float(k), temp)
        shrink = jnp.where(above, 0.5**k, shrink)
    column_ref[heavy_rows:base, :] = temp
    column_ref[press_base : press_base + levels, :] = cell * shrink - float(PRESS)
    tile = WIDE
    table = jnp.concatenate([table_lw_ref[...], table_sw_ref[...]], axis=0)
    solar_row[...] = jnp.zeros_like(solar_row)
    solar_row[:, 0:g_sw] = solar_ref[...]
    frac_lanes[...] = jnp.transpose(jnp.broadcast_to(frac_ref[...], (LANES, g_lw)))
    solar_lanes[...] = jnp.transpose(jnp.broadcast_to(solar_row[...], (LANES, WIDE)))
    weight_sum = jnp.sum(frac_ref[...])
    solar_sum = jnp.sum(solar_ref[...])

    def scalar(offset, count, cols):
        values = column_ref[base + offset : base + offset + 1, cols]
        for piece in range(1, count):
            values = values + column_ref[base + offset + piece : base + offset + piece + 1, cols]
        return values

    def column_tile(step, carry):
        cols = pl.ds(pl.multiple_of(step * tile, tile), tile)
        surface = scalar(0, 3, cols)
        cosine = scalar(3, 3, cols)
        albedo = scalar(6, 3, cols)
        lit = scalar(9, 1, cols) < DARK
        slant = -LOG2E / cosine
        entry = iota((PRESS, tile), 0)

        planck = planck_ref[:, cols]
        level_gap = jnp.zeros((1, tile), jnp.float32)
        steps = planck[:-1] - planck[1:]
        step_down[...] = jnp.concatenate([-planck[:1], steps, level_gap], axis=0)[:, None, :]
        step_up[...] = jnp.concatenate(
            [level_gap, -steps, surface - planck[-1:]], axis=0
        )[:, None, :]
        flux_ref[...] = jnp.broadcast_to(step_down[0], (g_lw, tile))
        beam_ref[...] = jnp.concatenate([solar_lanes[0:g_sw, :]] * 2, axis=1)

        def fold(values):
            return jnp.sum(values.reshape(-1, 8, values.shape[-1]), axis=0)

        def absorb_level(level, carry):
            frac = jnp.concatenate([frac_lanes[...]] * 2, axis=1)

            def row(first):
                return column_ref[pl.ds(first + level, 1), cols]

            w0, w1, w2, w3 = (row(k * levels) for k in range(4))
            press = row(press_base).astype(jnp.int32)
            temp = row(4 * levels)
            offset = entry - press
            zero = jnp.zeros((), jnp.float32)
            near = jnp.where(offset == 0, w0, jnp.where(offset == 1, w1, zero))
            wrap = offset == 1 - PRESS
            far = jnp.where(
                offset == 0, w2, jnp.where(offset == 1, w3, jnp.where(wrap, w1, zero))
            )
            last = jnp.where(wrap[0:16], w3, zero).astype(jnp.bfloat16)
            near = near.astype(jnp.bfloat16)
            far = far.astype(jnp.bfloat16)
            temp = jnp.broadcast_to(temp.astype(jnp.bfloat16), (16, tile))
            hits = [temp == jnp.full((), k, jnp.bfloat16) for k in range(TEMPS)]
            blank = jnp.zeros((16, tile), jnp.bfloat16)
            blocks = []
            for k in range(TEMPS):
                for sub in range(0, PRESS, 16):
                    rest = blank
                    if k >= 2 and sub == 0:
                        rest = jnp.where(hits[k - 2], last, rest)
                    if k >= 1:
                        rest = jnp.where(hits[k - 1], far[sub : sub + 16], rest)
                    blocks.append(jnp.where(hits[k], near[sub : sub + 16], rest))
            mixing = jnp.concatenate(blocks, axis=0)
            absorb = jnp.dot(table, mixing, preferred_element_type=jnp.float32)
            path = path_ref[pl.ds(level, 1), cols]
            cloud = cloud_ref[pl.ds(level, 1), cols]
            transmit = jnp.exp2(absorb[:g_lw] * (path * DIFFUSE) + cloud * DIFFUSE)
            long_t[level] = transmit
            passed = flux_ref[...] * transmit
            lw_down[level] = fold(passed * frac)
            flux_ref[...] = passed + step_down[level + 1]
            beam = beam_ref[...] * jnp.exp2(absorb[g_lw:] * (path * slant) + cloud * slant)
            sw_down[level] = fold(beam)
            beam_ref[...] = beam
            diffuse_t[level] = jnp.exp2(
                absorb[g_lw:] * (path * DIFFUSE) + cloud * DIFFUSE
            )
            return carry

        lax.fori_loop(0, levels, absorb_level, 0, unroll=8)

        for sums in (lw_up, sw_up):
            sums[...] = jnp.zeros_like(sums)
        quarter_lw, quarter_sw = g_lw // 4, g_sw // 4

        def fluxes(work, carry):
            quarter = work // 2
            half = work % 2
            lanes = pl.ds(pl.multiple_of(half * LANES, LANES), LANES)
            long_g = pl.ds(pl.multiple_of(quarter * quarter_lw, 8), quarter_lw)
            sun_g = pl.ds(pl.multiple_of(quarter * quarter_sw, 8), quarter_sw)
            frac = frac_lanes[long_g, :]

            def up(back, state):
                flux, beam = state
                level = levels - 1 - back
                passed = flux * long_t[level, long_g, lanes]
                beam = beam * diffuse_t[level, sun_g, lanes]
                lw_up[level, :, lanes] += fold(passed * frac)
                sw_up[level, :, lanes] += fold(beam)
                return passed + step_up[level, :, lanes], beam

            flux = jnp.broadcast_to(step_up[levels, :, lanes], (quarter_lw, LANES))
            lax.fori_loop(0, levels, up, (flux, beam_ref[sun_g, lanes]), unroll=8)
            return carry

        lax.fori_loop(0, 8, fluxes, 0)

        own = planck * weight_sum
        below = jnp.sum(lw_down[...], axis=1) + own
        above = jnp.sum(lw_up[...], axis=1) + own
        ground = surface * weight_sum
        entering_down = jnp.concatenate([jnp.zeros((1, tile), jnp.float32), below[:-1]], axis=0)
        entering_up = jnp.concatenate([above[1:], ground], axis=0)
        lw_ref[:, cols] = (entering_down - below) + (entering_up - above)

        beam = jnp.sum(sw_down[...], axis=1) * cosine
        reflect = albedo * cosine
        diffuse = jnp.sum(sw_up[...], axis=1) * reflect
        top = solar_sum * cosine
        arriving = jnp.concatenate([top, beam[:-1]], axis=0)
        rising = jnp.concatenate([diffuse[1:], albedo * beam[-1:]], axis=0)
        heat = (arriving - beam) + (rising - diffuse)
        sw_ref[:, cols] = jnp.where(lit, heat, 0.0)
        ground_ref[:, cols] = jnp.where(lit, (1.0 - albedo) * beam[-1:], 0.0)
        return carry

    lax.fori_loop(0, columns // tile, column_tile, 0)

    groups = surface_ref.shape[0]
    every = pl.ds(0, columns)
    slot_high = scalar(9, 1, every).astype(jnp.int32)
    slot_low = scalar(10, 1, every).astype(jnp.int32)
    dyn_row = span_ref[...] // row_slots[0]
    home = dyn_row * (row_slots[1] // LANES) + slot_high
    at_home = home == iota((groups, columns), 0)
    at_lane = hot(slot_low == iota((LANES, columns), 0))
    total = None
    for piece in pieces(ground_ref[...]):
        spread = jnp.where(at_home, piece.astype(jnp.float32), 0.0).astype(jnp.bfloat16)
        term = contract(spread, at_lane, ((1,), (1,)))
        total = term if total is None else total + term
    surface_ref[...] = total


def params(**more):
    return pltpu.CompilerParams(vmem_limit_bytes=56 * 1024 * 1024, **more)


def shape_of(shape, dtype):
    return jax.ShapeDtypeStruct(shape, dtype)


def body(
    planck_source, absorber_path, cloud_depth, span_map, surface_source, interp_index,
    interp_weight, sunlit, sw_slot, cos_zenith, albedo, table_lw, table_sw, planck_frac,
    solar_weight,
):
    levels, columns = planck_source.shape
    stripes = lax.axis_size("col")
    devices = lax.axis_size("dyn") * stripes
    capacity = 2 * columns // devices
    slots = devices * capacity
    span = span_map[None, :]
    folded = fold_rows(capacity)
    link = pltpu.SemaphoreType.DMA((devices,))
    place_anywhere = pl.BlockSpec(memory_space=pl.ANY)
    heavy, light, place = pl.pallas_call(
        functools.partial(exchange_kernel, devices, capacity),
        out_shape=(
            shape_of((devices, capacity, LANES), jnp.bfloat16),
            shape_of((devices, folded, LANES), jnp.bfloat16),
            shape_of((1, columns), jnp.int32),
        ),
        in_specs=[VMEM] * 8,
        out_specs=(place_anywhere, place_anywhere, VMEM),
        scratch_shapes=[
            pltpu.VMEM((WIDE, columns), jnp.bfloat16),
            pltpu.VMEM((slots, columns), jnp.bfloat16),
            pltpu.VMEM((devices, capacity, LANES), jnp.bfloat16),
            pltpu.VMEM((devices, folded, LANES), jnp.bfloat16),
            pltpu.VMEM((devices, 1, LANES), jnp.float32),
            pltpu.VMEM((devices, 1, LANES), jnp.float32),
            *[link] * 6,
            pltpu.SemaphoreType.DMA((2,)),
        ],
        compiler_params=params(collective_id=1, has_side_effects=True),
    )(
        span, interp_index, interp_weight.reshape(4 * levels, columns), surface_source[None, :],
        cos_zenith[None, :], albedo[None, :], sunlit[None, :], sw_slot[None, :],
    )
    g_lw, g_sw = table_lw.shape[0], table_sw.shape[0]
    sw_all = devices * (columns // 2)
    row_slots = (stripes * columns, stripes * (columns // 2))
    heating_lw, heating_sw, surface = pl.pallas_call(
        functools.partial(radiation_kernel, row_slots, capacity),
        out_shape=(
            shape_of((levels, columns), jnp.float32),
            shape_of((levels, columns), jnp.float32),
            shape_of((sw_all // LANES, LANES), jnp.float32),
        ),
        in_specs=[VMEM] * 11,
        out_specs=(VMEM,) * 3,
        scratch_shapes=[
            pltpu.VMEM((WIDE, columns), jnp.float32),
            pltpu.VMEM((g_lw, WIDE), jnp.float32),
            pltpu.VMEM((g_sw, WIDE), jnp.float32),
            pltpu.VMEM((levels, g_sw, WIDE), jnp.float32),
            pltpu.VMEM((levels, g_lw, WIDE), jnp.float32),
            *[pltpu.VMEM((levels, 8, WIDE), jnp.float32)] * 4,
            pltpu.VMEM((1, columns), jnp.float32),
            pltpu.VMEM((1, WIDE), jnp.float32),
            pltpu.VMEM((g_lw, LANES), jnp.float32),
            pltpu.VMEM((WIDE, LANES), jnp.float32),
            *[pltpu.VMEM((levels + 1, 1, WIDE), jnp.float32)] * 2,
        ],
        compiler_params=params(),
    )(
        heavy.reshape(slots, LANES), light.reshape(devices * folded, LANES), place, span, absorber_path, cloud_depth, planck_source, table_lw, table_sw,
        planck_frac[None, :], solar_weight[None, :],
    )
    sw_surface = collect(surface.reshape(devices, -1, LANES), 2)
    return heating_lw, heating_sw, sw_surface.reshape(columns // 2)


def solution(mesh):
    wide = P(None, AXES)
    flat = P(AXES)
    in_specs = (
        wide, wide, wide, flat, flat, wide, P(None, None, AXES), flat, flat, flat, flat,
        P(), P(), P(), P(),
    )
    out_specs = (wide, wide, flat)
    return jax.shard_map(body, mesh=mesh, in_specs=in_specs, out_specs=out_specs, check_vma=False)
```
